128 devices in a mesh: ctx: 8 (over x, core), tp: 16 (over y, z).
Axes of the slice: x: 4, y: 4, z: 4, core: 2. Of those that a mesh axis runs over, the one named last changes fastest.
Arguments:
- states: bfloat16 [16384, 4096], P('ctx', 'tp'), may hold values from -6 to 6
- picked: int32 [4096], P('ctx'), may hold values from 0 to 2047, as said below
- counts: int32 [8], P('ctx'), may hold values from 64 to 512, as said below
- norm_gain: bfloat16 [4096], P('tp'), may hold values from 0.099609375 to 1.8984375
- router_weight: bfloat16 [4096], P('tp'), may hold values from -0.09375 to 0.09375
- w_query: bfloat16 [4096, 4096], P(None, 'tp'), may hold values from -0.19 to 0.19
- w_key: bfloat16 [4096, 4096], P(None, 'tp'), may hold values from -1.16 to 1.16
- w_value: bfloat16 [4096, 4096], P(None, 'tp'), may hold values from -0.09375 to 0.09375
- w_out: bfloat16 [4096, 4096], P('tp'), may hold values from -1 to 1
- upstream: bfloat16 [16384, 4096], P('ctx', 'tp'), may hold values from -6 to 6
Outputs:
- mixed: bfloat16 [16384, 4096], P('ctx', 'tp')
- grad_states: bfloat16 [16384, 4096], P('ctx', 'tp')
- grad_query: float32 [4096, 4096], P('ctx', 'tp')
- grad_key: float32 [4096, 4096], P('ctx', 'tp')
- grad_value: float32 [4096, 4096], P('ctx', 'tp')
- grad_output_proj: float32 [4096, 4096], P(('tp', 'ctx'))
- grad_gain: float32 [4096], P('tp')
- grad_router: float32 [4096], P('tp')
The draws below stay inside these ranges and needn't reach their ends.
Inputs may be any that keep to these rules, and one draw needn't show every extreme that they name: `picked`: in the 512 slots of context shard c, the first counts[c] entries are distinct token indices of that shard in strictly ascending order; every later slot holds 2047 and is not live. `counts`: some context shard has exactly 512 picked tokens.
All inputs are finite; a program needn't handle non-finite values.
Results may differ from the reference program's by a relative error of at most 0.02.
Values may be sent and summed in bfloat16 or wider, within the bound.
A program may use at most 128 MiB of HBM per device.

```python
import jax
import jax.numpy as jnp
from jax import lax

D = 4096
HEADS = 32
HD = 128
TOK_DEV = 2048
CAP = 512
SEQ = 16384
PICKS = 4096
N_CTX = 8
N_TP = 16


def shard_counts(key):
    base = jax.random.randint(jax.random.fold_in(key, 11), (N_CTX,), CAP // 8, CAP * 3 // 4 + 1)
    fullest = jax.random.randint(jax.random.fold_in(key, 12), (), 0, N_CTX)
    return jnp.where(jnp.arange(N_CTX) == fullest, CAP, base).astype(jnp.int32)


def shared_query(key):
    return jnp.clip(jax.random.normal(jax.random.fold_in(key, 21), (D, D), jnp.float32), -6.0, 6.0)


def draw_counts(key, part):
    return shard_counts(key)


def draw_picked(key, part):
    shard_sizes = shard_counts(key)
    key = jax.random.fold_in(key, 3)
    shard_keys = jax.random.split(key, N_CTX)

    def one_shard(shard_key, shard_size):
        order = jax.random.permutation(shard_key, TOK_DEV)[:CAP].astype(jnp.int32)
        slots = jnp.arange(CAP, dtype=jnp.int32)
        ranked = jnp.sort(jnp.where(slots < shard_size, order, order + TOK_DEV))
        return jnp.where(slots < shard_size, ranked, TOK_DEV - 1)
    return jax.vmap(one_shard)(shard_keys, shard_sizes).reshape(N_CTX * CAP).astype(jnp.int32)


def draw_w_query(key, part):
    shared = shared_query(key)
    return (shared * (1.2 / 64.0)).astype(jnp.bfloat16)


def draw_w_key(key, part):
    key = jax.random.fold_in(key, 6)
    fresh = jnp.clip(jax.random.normal(jax.random.fold_in(key, 1), (D, D), jnp.float32), -6.0, 6.0)
    return (fresh * (1.2 / 64.0)).astype(jnp.bfloat16)


def steps_of(own_key, extent, shards, least, top_value):
    gain = 1.0
    for axis_at, shards_of in shards:
        heights = jax.random.uniform(jax.random.fold_in(jax.random.fold_in(own_key, 6), axis_at), (shards_of,), jnp.float32, least / len(shards), top_value / len(shards))
        gain = gain * jnp.repeat(jnp.exp(heights), extent[axis_at] // shards_of).reshape((-1,) + (1,) * (len(extent) - 1 - axis_at))
    return gain


def gaussian(stream_key, extent, scale, most, cuts=(), kind=jnp.bfloat16):
    level = steps_of(stream_key, extent, cuts, -0.22, 0.18) if cuts else 1.0
    array = jax.random.normal(stream_key, extent, jnp.float32) * scale * level
    return jnp.minimum(jnp.maximum(array, -most), most).astype(kind)


def setup_inputs(seed: int = 0) -> dict:
    splits = jax.random.split(jax.random.key(seed), 11)
    return {
        "states": gaussian(splits[0], (SEQ, D), 1.0, 6.0, ((0, 8), (1, 16))),
        "picked": draw_picked(jax.random.fold_in(splits[10], 71), 0),
        "counts": draw_counts(jax.random.fold_in(splits[10], 71), 0),
        "norm_gain": jnp.clip(1.0 + 0.18 * jax.random.normal(splits[3], (D,), jnp.float32), 0.099609375, 1.8984375).astype(jnp.bfloat16),
        "router_weight": gaussian(splits[4], (D,), D ** -0.5, 0.09375, ((0, 16),)),
        "w_query": draw_w_query(jax.random.fold_in(splits[10], 71), 0),
        "w_key": draw_w_key(jax.random.fold_in(splits[10], 71), 0),
        "w_value": gaussian(splits[7], (D, D), D ** -0.5, 0.09375, ((1, 16),)),
        "w_out": gaussian(splits[8], (D, D), 0.0625, 1.0, ((0, 16),)),
        "upstream": gaussian(splits[9], (SEQ, D), 1.0, 6.0, ((0, 8), (1, 16))),
    }


def rounded(value):
    return lax.optimization_barrier(value.astype(jnp.bfloat16)).astype(jnp.float32)

def shard_probs(query_block, key_heads, live_flat, first):
    query_pos = first + jnp.arange(CAP, dtype=jnp.int32)
    key_pos = jnp.arange(PICKS, dtype=jnp.int32)
    allowed = (key_pos[None, :] <= query_pos[:, None]) & live_flat[None, :]
    scores = jnp.einsum('qhd,khd->hqk', query_block.astype(jnp.float32), key_heads.astype(jnp.float32)) * HD ** (-0.5)
    scores = jnp.where(allowed[None], scores, -1e+30)
    highest = lax.optimization_barrier(jnp.max(scores, axis=-1, keepdims=True))
    lifted = jnp.exp(scores - highest)
    return (lifted / lax.optimization_barrier(jnp.sum(lifted, axis=-1, keepdims=True))).astype(jnp.bfloat16)

def reference(states, picked, counts, norm_gain, router_weight, w_query, w_key, w_value, w_out, upstream):
    local_width = D // N_TP
    slots = jnp.arange(CAP, dtype=jnp.int32)
    live_flat = (slots[None, :] < counts[:, None]).reshape(PICKS)
    positions = (jnp.arange(N_CTX, dtype=jnp.int32)[:, None] * TOK_DEV + picked.reshape(N_CTX, CAP)).reshape(PICKS)
    chosen_rows = states[positions]
    gate_value = jax.nn.sigmoid(jnp.dot(chosen_rows, router_weight, preferred_element_type=jnp.float32))
    live_gate = jnp.where(live_flat, gate_value, 0.0)
    rows_wide = chosen_rows.astype(jnp.float32)
    inverse = lax.rsqrt(lax.optimization_barrier(jnp.mean(rows_wide * rows_wide, axis=1)) + 1e-05)
    gain_wide = norm_gain.astype(jnp.float32)
    normed = (rows_wide * inverse[:, None] * gain_wide[None, :]).astype(jnp.bfloat16)
    queries = jnp.dot(normed, w_query, preferred_element_type=jnp.float32).astype(jnp.bfloat16)
    keys_all = jnp.dot(normed, w_key, preferred_element_type=jnp.float32).astype(jnp.bfloat16)
    values_all = jnp.dot(normed, w_value, preferred_element_type=jnp.float32).astype(jnp.bfloat16)
    query_heads = queries.reshape(PICKS, HEADS, HD)
    key_heads = keys_all.reshape(PICKS, HEADS, HD)
    value_heads = values_all.reshape(PICKS, HEADS, HD)
    attended_parts = []
    for shard in range(N_CTX):
        first = shard * CAP
        probs_block = shard_probs(query_heads[first:first + CAP], key_heads, live_flat, first)
        attended_parts.append(jnp.einsum('hqk,khd->qhd', probs_block.astype(jnp.float32), value_heads.astype(jnp.float32)).astype(jnp.bfloat16))
    attended = jnp.concatenate(attended_parts, axis=0).reshape(PICKS, D)
    block_out = jnp.zeros((PICKS, D), jnp.float32)
    for group in range(N_TP):
        lower = group * local_width
        block_out = block_out + rounded(jnp.dot(attended[:, lower:lower + local_width], w_out[lower:lower + local_width], preferred_element_type=jnp.float32))
    mixed = states.astype(jnp.float32).at[positions].add(live_gate[:, None] * block_out).astype(jnp.bfloat16)
    chosen_grad = upstream[positions].astype(jnp.float32)
    block_grad = (live_gate[:, None] * chosen_grad).astype(jnp.bfloat16)
    gate_grad = jnp.where(live_flat, lax.optimization_barrier(jnp.sum(chosen_grad * block_out, axis=1)) * gate_value * (1.0 - gate_value), 0.0)
    grad_output_proj = jnp.dot(attended.T, block_grad, preferred_element_type=jnp.float32)
    attended_grad = jnp.dot(block_grad, w_out.T, preferred_element_type=jnp.float32).astype(jnp.bfloat16)
    grad_heads = attended_grad.reshape(PICKS, HEADS, HD)
    query_parts = []
    key_sum = jnp.zeros((PICKS, HEADS, HD), jnp.float32)
    value_sum = jnp.zeros((PICKS, HEADS, HD), jnp.float32)
    for shard in range(N_CTX):
        first = shard * CAP
        query_block = query_heads[first:first + CAP]
        grad_block = grad_heads[first:first + CAP].astype(jnp.float32)
        prob_wide = shard_probs(query_block, key_heads, live_flat, first).astype(jnp.float32)
        prob_grad = jnp.einsum('qhd,khd->hqk', grad_block, value_heads.astype(jnp.float32))
        spread = lax.optimization_barrier(jnp.sum(prob_wide * prob_grad, axis=-1, keepdims=True))
        score_grad = (prob_wide * (prob_grad - spread) * HD ** (-0.5)).astype(jnp.bfloat16)
        score_wide = score_grad.astype(jnp.float32)
        query_parts.append(jnp.einsum('hqk,khd->qhd', score_wide, key_heads.astype(jnp.float32)).astype(jnp.bfloat16))
        key_sum = key_sum + rounded(jnp.einsum('hqk,qhd->khd', score_wide, query_block.astype(jnp.float32)))
        value_sum = value_sum + rounded(jnp.einsum('hqk,qhd->khd', prob_wide, grad_block))
    query_grad = jnp.concatenate(query_parts, axis=0).reshape(PICKS, D)
    key_grad = key_sum.astype(jnp.bfloat16).reshape(PICKS, D)
    value_grad = value_sum.astype(jnp.bfloat16).reshape(PICKS, D)
    normed_grad = jnp.zeros((PICKS, D), jnp.float32)
    for group in range(N_TP):
        lower = group * local_width
        upper = lower + local_width
        term = jnp.dot(query_grad[:, lower:upper], w_query[:, lower:upper].T, preferred_element_type=jnp.float32)
        term = term + jnp.dot(key_grad[:, lower:upper], w_key[:, lower:upper].T, preferred_element_type=jnp.float32)
        term = term + jnp.dot(value_grad[:, lower:upper], w_value[:, lower:upper].T, preferred_element_type=jnp.float32)
        normed_grad = normed_grad + rounded(term)
    grad_gain = lax.optimization_barrier(jnp.sum(normed_grad * rows_wide * inverse[:, None], axis=0))
    scaled_grad = normed_grad * gain_wide[None, :]
    row_dot = lax.optimization_barrier(jnp.sum(scaled_grad * rows_wide, axis=1))
    rows_grad = inverse[:, None] * scaled_grad - rows_wide * (inverse * inverse * inverse * row_dot / D)[:, None]
    rows_grad = rows_grad + gate_grad[:, None] * router_weight.astype(jnp.float32)[None, :]
    rows_grad = jnp.where(live_flat[:, None], rows_grad, 0.0)
    grad_router = lax.optimization_barrier(jnp.sum(gate_grad[:, None] * rows_wide, axis=0))
    grad_query = jnp.dot(normed.T, query_grad, preferred_element_type=jnp.float32)
    grad_key = jnp.dot(normed.T, key_grad, preferred_element_type=jnp.float32)
    grad_value = jnp.dot(normed.T, value_grad, preferred_element_type=jnp.float32)
    grad_states = upstream.astype(jnp.float32).at[positions].add(rows_grad).astype(jnp.bfloat16)
    return (mixed, grad_states, grad_query, grad_key, grad_value, grad_output_proj, grad_gain, grad_router)
```

```python
import math

import jax
import jax.numpy as jnp
from jax import lax
from jax.experimental import pallas as pl
from jax.experimental.pallas import tpu as pltpu
from jax.sharding import PartitionSpec as P

D = 4096
HD = 128
CAP = 512
F32 = jnp.float32
BF16 = jnp.bfloat16
MESH_ID = pl.DeviceIdType.MESH
SCALING = HD ** (-0.5)
EXP2_SCALE = SCALING * math.log2(math.e)
FAR = -1e30
LAST_LAST = (((1,), (1,)), ((), ()))
FIRST_FIRST = (((0,), (0,)), ((), ()))
HOPS = (2, 1, -1, 0)


def pick(i, values):
    out = values[-1]
    for k in range(len(values) - 2, -1, -1):
        out = jnp.where(i == k, values[k], out)
    return out


def steps(count, work, after):
    @pl.loop(0, count)
    def _(i):
        work(i)
        for k, acts in after.items():

            @pl.when(i == k)
            def _():
                for act, *arguments in acts:
                    act(*arguments)


def dot(a, b, dims=(((1,), (0,)), ((), ()))):
    return lax.dot_general(a, b, dims, preferred_element_type=F32)


class Place:
    def __init__(self):
        self.ctx = lax.axis_index("ctx")
        self.tp = lax.axis_index("tp")
        self.x, self.core = lax.div(self.ctx, 2), lax.rem(self.ctx, 2)
        self.y, self.z = lax.div(self.tp, 4), lax.rem(self.tp, 4)

    def tp_at(self, dy, dz):
        return lax.rem(self.y + dy + 4, 4) * 4 + lax.rem(self.z + dz + 4, 4)

    def ctx_at(self, dx, other=0):
        return lax.rem(self.x + dx + 4, 4) * 2 + lax.rem(self.core + other, 2)

    def near(self, axis, step):
        if axis == "y":
            return (self.ctx, self.tp_at(step, 0))
        if axis == "z":
            return (self.ctx, self.tp_at(0, step))
        if axis == "x":
            return (self.ctx_at(step), self.tp)
        return (self.ctx_at(0, 1), self.tp)

    def tp_peer(self, p):
        return (self.ctx, lax.rem(self.tp + p, 16))

    def ctx_peer(self, p):
        return (lax.rem(self.ctx + p, 8), self.tp)


def greet(partners):
    barrier = pltpu.get_barrier_semaphore()
    for partner in partners:
        pl.semaphore_signal(barrier, inc=1, device_id=partner, device_id_type=MESH_ID)


def meet(partners):
    pl.semaphore_wait(pltpu.get_barrier_semaphore(), len(partners))


def remote(src, dst, sems, at, where):
    return pltpu.make_async_remote_copy(
        src_ref=src,
        dst_ref=dst,
        send_sem=sems.at[0, at],
        recv_sem=sems.at[1, at],
        device_id=where,
        device_id_type=MESH_ID,
    )


def add_into(dst, *terms):
    rows = dst.shape[0]
    slab = min(rows, 128 if dst.shape[1] <= 1024 else 16)

    @pl.loop(0, rows // slab)
    def _(i):
        at = pl.ds(pl.multiple_of(i * slab, slab), slab)
        if len(terms) == 1:
            dst[at] = dst[at] + terms[0][at]
        else:
            total = dst[at].astype(F32)
            for term in terms:
                total = total + term[at].astype(F32)
            dst[at] = total.astype(dst.dtype)


def sum_to(out, *terms):
    rows = out.shape[0]
    slab = min(rows, 128 if out.shape[1] <= 1024 else 16)

    @pl.loop(0, rows // slab)
    def _(i):
        at = pl.ds(pl.multiple_of(i * slab, slab), slab)
        total = terms[0][at].astype(F32)
        for term in terms[1:]:
            total = total + term[at].astype(F32)
        out[at] = total.astype(out.dtype)


def torus_block(place, half, a, b):
    return place.tp_at(b, a) if half == 0 else place.tp_at(a, b)


class TorusGather:
    def __init__(self, place, buf, sems):
        self.place, self.buf, self.sems = place, buf, sems
        self.rows = buf.shape[2]

    def plan(self, half, number):
        axes = ("z", "y") if half == 0 else ("y", "z")
        if number < 4:
            a, b, step, part = ((0, 0, 1, None), (0, 0, -1, None), (-1, 0, 1, 0), (1, 0, -1, 1))[number]
            axis = axes[0]
        else:
            a = (0, -1, 1, 2)[(number - 4) // 4]
            b, step, part = ((0, 1, None), (0, -1, None), (-1, 1, 0), (1, -1, 1))[(number - 4) % 4]
            axis = axes[1]
        ref = self.buf.at[torus_block(self.place, half, a, b), half]
        if part is not None:
            ref = ref.at[pl.ds(part * (self.rows // 2), self.rows // 2)]
        return remote(ref, ref, self.sems, half * 20 + number, self.place.near(axis, step))

    def start(self, *numbers):
        for number in numbers:
            for half in (0, 1):
                self.plan(half, number).start()

    def arrive(self, *numbers):
        for number in numbers:
            for half in (0, 1):
                self.plan(half, number).wait_recv()

    def pass_on(self, *pairs):
        for come, go in pairs:
            for half in (0, 1):
                self.plan(half, come).wait_recv()
                self.plan(half, go).start()

    def stage0(self):
        self.start(0, 1, 4, 5)

    def stage1(self):
        self.pass_on((0, 2), (1, 3))
        self.start(8, 9, 12, 13)

    def stage2(self):
        self.pass_on((4, 6), (5, 7))

    def stage3(self):
        self.arrive(2, 3)
        self.start(16, 17)

    def stage4(self):
        self.pass_on((8, 10), (9, 11), (12, 14), (13, 15))

    def stage5(self):
        self.pass_on((16, 18), (17, 19))

    def stage6(self):
        self.arrive(6, 7, 10, 11, 14, 15, 18, 19)

    def finish(self):
        for number in range(20):
            for half in (0, 1):
                self.plan(half, number).wait_send()


class TorusScatter:
    def __init__(self, place, part, small, big, sems):
        self.place, self.part, self.small, self.big, self.sems = place, part, small, big, sems

    def term(self, half, i, b):
        a, c = (HOPS[i], b) if i < 4 else (b, 0)
        return self.part.at[torus_block(self.place, half, a, c), half]

    def plan(self, half, i, k):
        axes = ("z", "y") if half == 0 else ("y", "z")
        axis = axes[1] if i < 4 else axes[0]
        step = 1 if k % 2 == 0 else -1
        if k < 2:
            src = self.term(half, i, 2)
            rows = src.shape[0] // 2
            src = src.at[pl.ds(k * rows, rows)]
            dst = self.small.at[half, i, k]
        else:
            src = self.term(half, i, step)
            dst = self.big.at[half, i, k - 2]
        return remote(src, dst, self.sems, half * 20 + i * 4 + k, self.place.near(axis, step))

    def far(self, *rounds):
        for i in rounds:
            for half in (0, 1):
                self.plan(half, i, 0).start()
                self.plan(half, i, 1).start()

    def middle(self, *rounds):
        for i in rounds:
            for half in (0, 1):
                for k, step in ((0, 1), (1, -1)):
                    self.plan(half, i, k).wait_recv()
                    term = self.term(half, i, step)
                    rows = term.shape[0] // 2
                    add_into(term.at[pl.ds(k * rows, rows)], self.small.at[half, i, k])
                    self.plan(half, i, 2 + k).start()

    def near(self, *rounds):
        for i in rounds:
            for half in (0, 1):
                self.plan(half, i, 2).wait_recv()
                self.plan(half, i, 3).wait_recv()
                add_into(self.term(half, i, 0), self.big.at[half, i, 0], self.big.at[half, i, 1])

    def last(self, out):
        for half in (0, 1):
            self.plan(half, 4, 2).wait_recv()
            self.plan(half, 4, 3).wait_recv()
            rows = self.part.shape[2]
            sum_to(
                out.at[pl.ds(half * rows, rows)],
                self.term(half, 4, 0), self.big.at[half, 4, 0], self.big.at[half, 4, 1],
            )

    def finish(self):
        for i in range(5):
            for half in (0, 1):
                for k in range(4):
                    self.plan(half, i, k).wait_send()


class ContextGather:
    def __init__(self, place, buf, cut, sems):
        self.place, self.buf, self.cut, self.sems = place, buf, cut, sems

    def plan(self, k):
        hop, axis, step, part = (
            (0, "core", 0, None), (0, "x", 1, None), (0, "x", -1, None),
            (-1, "x", 1, 0), (1, "x", -1, 1),
            (-1, "core", 0, None), (1, "core", 0, None), (2, "core", 0, None),
        )[k]
        ref = self.buf.at[self.place.ctx_at(hop)]
        if part is not None:
            ref = ref.at[pl.ds(0, self.cut) if part == 0 else pl.ds(self.cut, ref.shape[0] - self.cut)]
        return remote(ref, ref, self.sems, k, self.place.near(axis, step))

    def start(self, *numbers):
        for k in numbers:
            self.plan(k).start()

    def arrive(self, *numbers):
        for k in numbers:
            self.plan(k).wait_recv()

    def finish(self):
        for k in range(8):
            self.plan(k).wait_send()


class ContextScatter:
    def __init__(self, place, part, sib, small, big, sems):
        self.place, self.part, self.sib, self.small, self.big, self.sems = (
            place, part, sib, small, big, sems
        )

    def plan(self, k):
        place = self.place
        if k < 4:
            return self.sibling(k)
        step = 1 if k % 2 == 0 else -1
        if k < 6:
            src = self.part.at[place.ctx_at(2)]
            rows = src.shape[0] // 2
            src = src.at[pl.ds((k - 4) * rows, rows)]
            dst = self.small.at[k - 4]
        else:
            src = self.part.at[place.ctx_at(step)]
            dst = self.big.at[k - 6]
        return remote(src, dst, self.sems, k, place.near("x", step))

    def sibling(self, k):
        src = self.part.at[self.place.ctx_at(pick(k, HOPS), 1)]
        return remote(src, self.sib.at[k], self.sems, k, self.place.near("core", 0))

    def give(self, *hops):
        for k in hops:
            self.sibling(k).start()

    def take(self, *hops):
        for k in hops:
            self.sibling(k).wait_recv()
            add_into(self.part.at[self.place.ctx_at(pick(k, HOPS))], self.sib.at[k])

    def take_all(self):
        @pl.loop(0, 4)
        def _(k):
            self.take(k)

    def far(self):
        self.plan(4).start()
        self.plan(5).start()

    def near(self, *sides):
        for side in sides:
            k, step = ((4, 1), (5, -1))[side]
            self.plan(k).wait_recv()
            term = self.part.at[self.place.ctx_at(step)]
            rows = term.shape[0] // 2
            add_into(term.at[pl.ds((k - 4) * rows, rows)], self.small.at[k - 4])
            self.plan(k + 2).start()

    def last(self, out):
        self.plan(6).wait_recv()
        self.plan(7).wait_recv()
        sum_to(out, self.part.at[self.place.ctx_at(0)], self.big.at[0], self.big.at[1])

    def finish(self):
        for k in range(8):
            self.plan(k).wait_send()


class Exchange:
    def __init__(self, me, peer, count, buf, sems):
        self.me, self.peer, self.count, self.buf, self.sems = me, peer, count, buf, sems

    def plan(self, p):
        ref = self.buf.at[self.me]
        return remote(ref, ref, self.sems, p - 1, self.peer(p))

    def start(self):
        for p in range(1, self.count):
            self.plan(p).start()

    def total(self):
        for p in range(1, self.count):
            self.plan(p).wait_recv()
        return jnp.sum(self.buf[...], axis=0)

    def finish(self):
        for p in range(1, self.count):
            self.plan(p).wait_send()


def to_packed(first, second):
    lane = lax.broadcasted_iota(jnp.int32, (CAP, 128), 1)
    both = jnp.where(lane % 2 == 0, first, second).T
    return jnp.concatenate([pack(both[0:1]), pack(both[1:2])], axis=0)


def to_columns(rows):
    return jnp.concatenate([rows] * 16, axis=0).T


def pack(row):
    return jnp.concatenate([row[:, 128 * i : 128 * (i + 1)] for i in range(4)], axis=0)


def unpack(lines):
    row = jnp.concatenate([lines[i : i + 1] for i in range(4)], axis=1)
    return jnp.broadcast_to(row, (8, CAP))


SPOT_HOPS = (2, 2, 1, -1, 1, -1, 0, 0)
SPOT_CORES = (1, 0, 1, 1, 0, 0, 1, 0)


class Refs:
    pass


def gather_rows(r, staged, picked_columns, out):
    def chunk(i):
        token = lax.broadcasted_iota(jnp.int32, (CAP, CAP), 1) + i * CAP
        hit = jnp.where(picked_columns == token.astype(F32), 1.0, 0.0).astype(BF16)
        return dot(hit, r.part[staged + i].reshape(CAP, 256))

    out[...] = ((chunk(0) + chunk(1)) + (chunk(2) + chunk(3))).astype(BF16).reshape(2, 256, 256)


def scatter_rows(r, staged, goal, rows, hbm, sems, first):
    slot = lax.broadcasted_iota(jnp.int32, (1, CAP), 1)
    picked = jnp.where(slot < r.counts[0], r.picked[...].reshape(1, CAP), -1)

    @pl.loop(0, 4)
    def _(i):
        for half in range(2):
            if first:
                token = lax.broadcasted_iota(jnp.int32, (256, CAP), 0) + (i * CAP + half * 256)
                hit = jnp.where(picked == token, 1.0, 0.0)
                r.kv[2 * i + half, 0:256] = hit.astype(BF16)
                any_hit = jnp.max(hit, axis=1, keepdims=True) > 0.0
                for base in (staged + i, 4 + i):
                    old = r.bgrad[base, half].astype(F32)
                    r.bgrad[base, half] = jnp.where(any_hit, 0.0, old).astype(BF16)
            new = dot(r.kv[2 * i + half, 0:256], rows[...])
            r.bgrad[goal + i, half] = (r.bgrad[staged + i, half].astype(F32) + new).astype(BF16)
        pltpu.make_async_copy(r.bgrad.at[goal + i], hbm.at[i], sems.at[i]).start()


def forward_phase(place, r, partners):
    tp, ctx = place.tp, place.ctx
    picked_row = jnp.broadcast_to(r.picked[...].reshape(1, CAP).astype(F32), (8, CAP))
    picked_columns = to_columns(picked_row)[:, 0:1]
    r.stage_loads[0].wait()
    gather_rows(r, 0, picked_columns, r.rows)
    rows3 = r.rows[...].astype(F32).reshape(CAP, 256)
    gain = r.gain[...].astype(F32).reshape(1, 256)
    router = r.router[...].astype(F32).reshape(1, 256)
    r.normed[tp] = (rows3 * gain).astype(BF16).reshape(2, 256, 256)
    meet(partners)
    rows_in = TorusGather(place, r.normed, r.normed_sems)
    rows_in.stage0()

    stats = Exchange(tp, place.tp_peer, 16, r.stat_buf, r.stat_sems)
    squares = jnp.sum(rows3 * rows3, axis=1, keepdims=True)
    logits = jnp.sum(rows3 * router, axis=1, keepdims=True)
    r.stat_buf[tp] = to_packed(squares, logits)
    stats.start()
    r.stage_loads[1].wait()
    gather_rows(r, 4, picked_columns, r.uprows)
    r.bgrad[tp] = r.uprows[...]
    r.grads_in = grads_in = TorusGather(place, r.bgrad, r.bgrad_sems)

    def project(i):
        b = pick(i, (0, -1, 1, 2))
        for half in (0, 1):
            rows = pl.ds(half * 256, 256)
            terms = []
            for a in range(4):
                t = torus_block(place, half, a, b)
                terms.append(dot(r.normed[t, half], r.w_in[t]))
            term = (terms[0] + terms[1]) + (terms[2] + terms[3])
            r.acc[rows] = jnp.where(i == 0, term, r.acc[rows] + term)

    rows_in.stage1()
    rows_in.stage2()
    rows_in.stage3()
    for load in r.loads:
        load.wait()
    steps(
        4, project,
        {0: [(rows_in.stage4,), (rows_in.stage5,), (grads_in.stage0,)], 2: [(rows_in.stage6,)]},
    )
    total = stats.total()
    inverse = lax.rsqrt(to_columns(unpack(total[0:4]))[:, 0:1] * (1.0 / D) + 1e-05)
    gate = jax.nn.sigmoid(to_columns(unpack(total[4:8]))[:, 0:1])
    slot = lax.broadcasted_iota(jnp.int32, (CAP, 1), 0)
    r.inverse[...] = jnp.broadcast_to(inverse, (CAP, 128))
    r.gate[...] = jnp.broadcast_to(gate, (CAP, 128))
    r.live_gate[...] = jnp.broadcast_to(jnp.where(slot < r.counts[0], gate, 0.0), (CAP, 128))
    r.kv[ctx, pl.ds(0, CAP)] = (r.acc[:, 256:768] * inverse).astype(BF16)
    count = r.counts[0]
    high = lax.div(count, 256) * 256
    line = lax.broadcasted_iota(jnp.int32, (16, CAP), 0)
    r.kv[ctx, pl.ds(CAP, 16)] = jnp.where(
        line == 0, high.astype(F32), jnp.where(line == 1, (count - high).astype(F32), 0.0)
    ).astype(BF16)
    keys_in = ContextGather(place, r.kv, 272, r.kv_sems)
    keys_in.start(0, 1, 2)
    r.q[...] = (r.acc[:, 0:256] * inverse).astype(BF16)
    grads_in.stage1()

    for head in range(2):
        r.high[head] = jnp.full((8, CAP), FAR, F32)
        r.mass[head] = jnp.zeros((8, CAP), F32)
        r.out_t[head] = jnp.zeros((HD, CAP), F32)

    def attend(c):
        marks = r.kv[c, pl.ds(CAP, 16)].astype(F32)
        query = lax.broadcasted_iota(jnp.int32, (1, CAP), 1) + ((ctx - c) * CAP + 1)
        limit = jnp.minimum(marks[0:1] + marks[1:2], query.astype(F32))
        allowed = lax.broadcasted_iota(jnp.int32, (CAP, CAP), 0).astype(F32) < limit
        for head in range(2):
            keys = r.kv[c, 0:CAP, head * HD : (head + 1) * HD]
            values = r.kv[c, 0:CAP, 256 + head * HD : 256 + (head + 1) * HD]
            scores = dot(keys, r.q[:, head * HD : (head + 1) * HD], LAST_LAST)
            scores = jnp.where(allowed, scores, FAR)
            before = r.high[head][0:1]
            high = jnp.maximum(before, jnp.max(scores, axis=0, keepdims=True))
            fade = jnp.exp2((before - high) * EXP2_SCALE)
            lifted = jnp.exp2((scores - high) * EXP2_SCALE)
            r.high[head] = jnp.broadcast_to(high, (8, CAP))
            mass = r.mass[head][0:1] * fade + jnp.sum(lifted, axis=0, keepdims=True)
            r.mass[head] = jnp.broadcast_to(mass, (8, CAP))
            r.out_t[head] = r.out_t[head] * fade + dot(values, lifted.astype(BF16), FIRST_FIRST)

    def attend_step(i):
        c = place.ctx_at(pick(i, (0, 0, -1, 1, -1, 1, 2, 2)), pick(i, (0, 1, 0, 0, 1, 1, 0, 1)))

        @pl.when(c <= ctx)
        def _():
            attend(c)

    steps(
        8, attend_step,
        {
            0: [(grads_in.stage2,), (grads_in.stage3,), (keys_in.arrive, 0)],
            1: [
                (grads_in.stage4,),
                (keys_in.arrive, 1), (keys_in.start, 3, 5),
                (keys_in.arrive, 2), (keys_in.start, 4, 6),
            ],
            3: [(grads_in.stage5,), (keys_in.arrive, 5, 6)],
            4: [(keys_in.arrive, 3, 4), (keys_in.start, 7)],
            6: [(keys_in.arrive, 7)],
        },
    )
    for head in range(2):
        out = (r.out_t[head] * (1.0 / r.mass[head][0:1])).T
        r.attended[:, head * HD : (head + 1) * HD] = out.astype(BF16)
    rows_in.finish()
    stats.finish()
    keys_in.finish()


def backward_phase(place, r):
    tp, ctx = place.tp, place.ctx
    out_sum = TorusScatter(place, r.part, r.out_small, r.out_big, r.out_sems)

    def project_out(i):
        b = pick(i, (2, 1, -1, 0))
        for half in (0, 1):
            for a in range(4):
                t = torus_block(place, half, a, b)
                cols = pl.ds(pl.multiple_of(t * 256, 256), 256)
                r.part[t, half] = dot(
                    r.attended[half * 256 : (half + 1) * 256], r.w_out[:, cols]
                ).astype(BF16)

    steps(4, project_out, {0: [(out_sum.far, 0, 1, 2, 3)]})
    r.grads_in.stage6()

    live_gate = r.live_gate[:, 0:1]
    r.grads[:, 0:256] = (r.attended[...].astype(F32) * live_gate).astype(BF16)
    r.acc[:, 0:256] = jnp.zeros((CAP, 256), F32)

    @pl.loop(0, 16, unroll=4)
    def _(t):
        cols = pl.ds(pl.multiple_of(t * 256, 256), 256)
        piece = r.bgrad[t].reshape(CAP, 256)
        r.acc[:, 0:256] += dot(piece, r.w_out[:, cols], LAST_LAST)
        term = dot(r.grads[:, 0:256], piece, FIRST_FIRST)
        r.wo_part[:, :, cols] = term.astype(BF16).reshape(8, 32, 256)

    wo_sum = ContextScatter(place, r.wo_part, r.wo_sib, r.wo_small, r.wo_big, r.wo_sems)
    wo_sum.give(0, 1, 2, 3)
    r.agrad[...] = (r.acc[:, 0:256] * live_gate).astype(BF16)
    r.grads_in.finish()
    for load in r.base_loads:
        load.start()
    for head in range(2):
        cols = slice(head * HD, (head + 1) * HD)
        product = r.agrad[:, cols].astype(F32) * r.attended[:, cols].astype(F32)
        r.spread[head] = jnp.broadcast_to(jnp.sum(product.T, axis=0, keepdims=True), (8, CAP))
        r.high[head] = r.high[head] * EXP2_SCALE + jnp.log2(r.mass[head])
        r.out_t[head] = jnp.zeros((HD, CAP), F32)

    def attend_back(c):
        marks = r.kv[c, pl.ds(CAP, 16)].astype(F32)
        query = lax.broadcasted_iota(jnp.int32, (1, CAP), 1) + ((ctx - c) * CAP + 1)
        limit = jnp.minimum(marks[0:1] + marks[1:2], query.astype(F32))
        allowed = lax.broadcasted_iota(jnp.int32, (CAP, CAP), 0).astype(F32) < limit
        for head in range(2):
            cols = slice(head * HD, (head + 1) * HD)
            keys = r.kv[c, 0:CAP, head * HD : (head + 1) * HD]
            values = r.kv[c, 0:CAP, 256 + head * HD : 256 + (head + 1) * HD]
            queries, grads = r.q[:, cols], r.agrad[:, cols]
            scores = dot(keys, queries, LAST_LAST)
            scores = jnp.where(allowed, scores, FAR)
            probs = jnp.exp2(scores * EXP2_SCALE - r.high[head][0:1])
            prob_grad = dot(values, grads, LAST_LAST)
            score_grad = (probs * (prob_grad - r.spread[head][0:1])).astype(BF16)
            r.kv_part[c, :, 256 + head * HD : 256 + (head + 1) * HD] = dot(
                probs.astype(BF16), grads
            ).astype(BF16)
            r.kv_part[c, :, head * HD : (head + 1) * HD] = (
                dot(score_grad, queries) * SCALING
            ).astype(BF16)
            r.out_t[head] = r.out_t[head] + dot(keys, score_grad, FIRST_FIRST)

    def back_step(i):
        c = place.ctx_at(pick(i, SPOT_HOPS), pick(i, SPOT_CORES))

        @pl.when(c <= ctx)
        def _():
            attend_back(c)

        @pl.when(c > ctx)
        def _():
            r.kv_part[c] = jnp.zeros((CAP, CAP), BF16)

    kv_sum = ContextScatter(place, r.kv_part, r.kv_sib, r.kv_small, r.kv_big, r.kv_grad_sems)
    steps(
        8, back_step,
        {
            0: [(kv_sum.give, 0), (out_sum.middle, 0, 1, 2, 3)],
            1: [(kv_sum.take, 0), (kv_sum.far,)],
            2: [(kv_sum.give, 1), (wo_sum.take_all,), (wo_sum.far,)],
            3: [(kv_sum.give, 2)],
            4: [(kv_sum.take, 1), (kv_sum.near, 0)],
            5: [(kv_sum.take, 2), (kv_sum.near, 1), (wo_sum.near, 0, 1)],
            6: [(kv_sum.give, 3), (out_sum.near, 0), (out_sum.far, 4)],
            7: [(out_sum.near, 1, 2), (out_sum.middle, 4)],
        },
    )
    for head in range(2):
        r.grads[:, head * HD : (head + 1) * HD] = (r.out_t[head] * SCALING).T.astype(BF16)
    kv_sum.take(3)
    out_sum.near(3)

    def weight_term(part, lower, upper, c):
        pair = [r.normed[c * 2 + i].reshape(CAP, 256) for i in range(2)]
        term = dot(jnp.concatenate(pair, axis=1), r.scaled[:, lower:upper], FIRST_FIRST)
        part[c] = term.astype(BF16)

    inverse = r.inverse[:, 0:1]
    r.scaled[:, 0:256] = (r.grads[:, 0:256].astype(F32) * inverse).astype(BF16)
    wq_sum = ContextScatter(place, r.wq_part, r.wq_sib, r.wq_small, r.wq_big, r.wq_sems)

    def query_step(i):
        weight_term(r.wq_part, 0, 256, place.ctx_at(pick(lax.rem(i, 4), HOPS), 1 - lax.div(i, 4)))

        @pl.when(i < 4)
        def _():
            wq_sum.give(i)

    steps(8, query_step, {})
    wq_sum.take_all()
    wq_sum.far()

    out_sum.last(r.wide)
    block_out = r.wide[...]
    rows3 = r.rows[...].astype(F32).reshape(CAP, 256)
    chosen_grad = r.uprows[...].astype(F32).reshape(CAP, 256)
    r.mixed_rows[...] = (rows3 + live_gate * block_out).astype(BF16)
    gates = Exchange(tp, place.tp_peer, 16, r.gate_buf, r.gate_sems)
    gate_part = jnp.sum(chosen_grad * block_out, axis=1, keepdims=True)
    r.gate_buf[tp] = to_packed(gate_part, gate_part)
    gates.start()

    kv_sum.last(r.grads.at[:, pl.ds(256, 512)])
    r.scaled[:, 256:768] = (r.grads[:, 256:768].astype(F32) * inverse).astype(BF16)
    out_sum.finish()
    kv_sum.finish()
    norm_sum = TorusScatter(place, r.part, r.norm_small, r.norm_big, r.norm_sems)

    def project_back(i):
        b = pick(i, (2, 1, -1, 0))
        for half in (0, 1):
            for a in range(4):
                t = torus_block(place, half, a, b)
                r.part[t, half] = dot(
                    r.grads[half * 256 : (half + 1) * 256], r.w_in[t], LAST_LAST
                ).astype(BF16)

    steps(4, project_back, {0: [(norm_sum.far, 0, 1, 2, 3)], 2: [(wq_sum.near, 0, 1)]})

    dot_part = jnp.sum(r.grads[:, 0:256].astype(F32) * r.q[...].astype(F32), axis=1, keepdims=True)
    dot_part = dot_part + jnp.sum(
        r.grads[:, 256:768].astype(F32) * r.kv[ctx, 0:CAP, :].astype(F32), axis=1, keepdims=True
    )
    dot_part = dot_part / inverse
    dots = Exchange(tp, place.tp_peer, 16, r.dot_buf, r.dot_sems)
    r.dot_buf[tp] = to_packed(dot_part, dot_part)
    dots.start()
    wkv_sum = ContextScatter(place, r.kv_part, r.wkv_sib, r.wkv_small, r.wkv_big, r.wkv_sems)

    def key_value_step(i):
        c = place.ctx_at(pick(i, SPOT_HOPS), pick(i, SPOT_CORES))
        weight_term(r.kv_part, 256, 768, c)

    steps(
        8, key_value_step,
        {
            0: [(wkv_sum.give, 0), (norm_sum.middle, 0, 1, 2, 3)],
            1: [(wkv_sum.take, 0), (wkv_sum.far,)],
            2: [(wkv_sum.give, 1)],
            3: [(wkv_sum.give, 2)],
            4: [(wkv_sum.take, 1), (wkv_sum.near, 0)],
            5: [(wkv_sum.take, 2), (wkv_sum.near, 1), (norm_sum.near, 0), (norm_sum.far, 4)],
            6: [(wkv_sum.give, 3)],
        },
    )
    for load in r.base_loads:
        load.wait()
    scatter_rows(r, 0, 8, r.mixed_rows, r.o_mixed, r.mixed_sems, True)
    norm_sum.near(1, 2)
    norm_sum.middle(4)
    wkv_sum.take(3)
    norm_sum.near(3)
    wo_sum.last(r.grad_out)
    r.out_copy("grad_out", r.grad_out, r.o_grad_out)
    wq_sum.last(r.grad_q)
    r.out_copy("grad_q", r.grad_q, r.o_grad_q)

    gate_dot = to_columns(unpack(gates.total()[0:4]))[:, 0:1]
    row_dot = to_columns(unpack(dots.total()[0:4]))[:, 0:1]
    slot = lax.broadcasted_iota(jnp.int32, (CAP, 1), 0)
    alive = slot < r.counts[0]
    gate = r.gate[:, 0:1]
    gate_grad = jnp.where(alive, gate_dot * gate * (1.0 - gate), 0.0)
    router_part = jnp.sum(gate_grad * rows3, axis=0, keepdims=True)
    gain = r.gain[...].astype(F32).reshape(1, 256)
    router = r.router[...].astype(F32).reshape(1, 256)
    known = gate_grad * router - rows3 * (inverse * inverse * inverse * row_dot * (1.0 / D))
    norm_sum.last(r.wide)
    normed_grad = r.wide[...]
    sums = Exchange(ctx, place.ctx_peer, 8, r.sum_buf, r.sum_sems)
    gain_part = jnp.sum(normed_grad * rows3 * inverse, axis=0, keepdims=True)
    line = lax.broadcasted_iota(jnp.int32, (8, 256), 0)
    r.sum_buf[ctx] = jnp.where(line == 0, gain_part, router_part)
    sums.start()
    rows_grad = jnp.where(alive, inverse * (normed_grad * gain) + known, 0.0)
    r.grad_rows[...] = (chosen_grad + rows_grad).astype(BF16)
    scatter_rows(r, 4, 12, r.grad_rows, r.o_grad_states, r.states_sems, False)
    wkv_sum.last(r.grad_kv)
    r.out_copy("grad_k", r.acc.at[:, pl.ds(256, 256)], r.o_grad_k)
    r.out_copy("grad_v", r.acc.at[:, pl.ds(512, 256)], r.o_grad_v)
    r.o_small[...] = sums.total()
    for each in (wo_sum, wq_sum, wkv_sum, norm_sum, gates, dots, sums):
        each.finish()


DMA = pltpu.SemaphoreType.DMA


def vm(shape, dtype):
    return pltpu.VMEM(shape, dtype)


def scatter_scratch(name, rows, cols):
    return {
        name + "_part": vm((8, rows, cols), BF16),
        name + "_sib": vm((4, rows, cols), BF16),
        name + "_small": vm((2, rows // 2, cols), BF16),
        name + "_big": vm((2, rows, cols), BF16),
    }


def scratch_table():
    table = {
        "normed": vm((16, 2, 256, 256), BF16),
        "bgrad": vm((16, 2, 256, 256), BF16),
        "part": vm((16, 2, 256, 256), BF16),
        "kv": vm((8, CAP + 16, CAP), BF16),
        "w_in": vm((16, 256, 768), BF16),
        "w_out": vm((256, D), BF16),
        "acc": vm((CAP, 768), F32),
        "wide": vm((CAP, 256), F32),
        "q": vm((CAP, 256), BF16),
        "attended": vm((CAP, 256), BF16),
        "agrad": vm((CAP, 256), BF16),
        "grads": vm((CAP, 768), BF16),
        "high": vm((2, 8, CAP), F32),
        "mass": vm((2, 8, CAP), F32),
        "spread": vm((2, 8, CAP), F32),
        "out_t": vm((2, HD, CAP), F32),
        "inverse": vm((CAP, 128), F32),
        "live_gate": vm((CAP, 128), F32),
        "gate": vm((CAP, 128), F32),
        "stat_buf": vm((16, 8, 128), F32),
        "gate_buf": vm((16, 8, 128), F32),
        "dot_buf": vm((16, 8, 128), F32),
        "sum_buf": vm((8, 8, 256), F32),
        "out_small": vm((2, 5, 2, 128, 256), BF16),
        "out_big": vm((2, 5, 2, 256, 256), BF16),
        "norm_small": vm((2, 5, 2, 128, 256), BF16),
        "norm_big": vm((2, 5, 2, 256, 256), BF16),
        "rows": vm((2, 256, 256), BF16),
        "uprows": vm((2, 256, 256), BF16),
        "scaled": vm((CAP, 768), BF16),
        "mixed_rows": vm((CAP, 256), BF16),
        "grad_rows": vm((CAP, 256), BF16),
        "grad_out": vm((32, D), F32),
        "stage_sems": DMA((4,)),
        "mixed_sems": DMA((4,)),
        "states_sems": DMA((4,)),
        "out_copy_sems": DMA((4,)),
        "load_sems": DMA((4,)),
        "stat_sems": DMA((2, 15)),
        "gate_sems": DMA((2, 15)),
        "dot_sems": DMA((2, 15)),
        "sum_sems": DMA((2, 7)),
        "normed_sems": DMA((2, 40)),
        "bgrad_sems": DMA((2, 40)),
        "out_sems": DMA((2, 40)),
        "norm_sems": DMA((2, 40)),
        "kv_sems": DMA((2, 8)),
        "kv_grad_sems": DMA((2, 8)),
        "wo_sems": DMA((2, 8)),
        "wq_sems": DMA((2, 8)),
        "wkv_sems": DMA((2, 8)),
    }
    table.update(scatter_scratch("kv", CAP, CAP))
    table.update(scatter_scratch("wo", 32, D))
    table.update(scatter_scratch("wq", CAP, 256))
    table.update(scatter_scratch("wkv", CAP, CAP))
    del table["wkv_part"]
    return table


INPUTS = (
    "picked", "gain", "router", "counts", "states", "upstream", "w_query", "w_key", "w_value", "w_output",
)
OUTPUTS = {
    "o_mixed": ((4, 2, 256, 256), BF16),
    "o_grad_states": ((4, 2, 256, 256), BF16),
    "o_grad_q": ((CAP, 256), F32),
    "o_grad_k": ((CAP, 256), F32),
    "o_grad_v": ((CAP, 256), F32),
    "o_grad_out": ((32, D), F32),
    "o_small": ((8, 256), F32),
}
COPIES = ("grad_out", "grad_q", "grad_k", "grad_v")


def layer_kernel(*refs):
    r = Refs()
    names = list(INPUTS) + list(OUTPUTS) + list(scratch_table())
    for name, ref in zip(names, refs, strict=True):
        setattr(r, name, ref)
    r.grad_q = r.acc.at[:, pl.ds(0, 256)]
    r.grad_kv = r.acc.at[:, pl.ds(256, CAP)]
    place = Place()
    r.stage_loads = [
        pltpu.make_async_copy(src, r.part.at[pl.ds(4 * i, 4)], r.stage_sems.at[i])
        for i, src in enumerate((r.states, r.upstream))
    ]
    r.base_loads = [
        pltpu.make_async_copy(src, r.bgrad.at[pl.ds(4 * i, 4)], r.stage_sems.at[2 + i])
        for i, src in enumerate((r.states, r.upstream))
    ]
    r.loads = [
        pltpu.make_async_copy(w, r.w_in.at[:, :, pl.ds(256 * i, 256)], r.load_sems.at[i])
        for i, w in enumerate((r.w_query, r.w_key, r.w_value))
    ]
    r.loads.append(pltpu.make_async_copy(r.w_output, r.w_out, r.load_sems.at[3]))
    out_copies = []

    def out_copy(name, src, dst):
        copy = pltpu.make_async_copy(src, dst, r.out_copy_sems.at[COPIES.index(name)])
        copy.start()
        out_copies.append(copy)

    r.out_copy = out_copy
    partners = [place.tp_peer(p) for p in range(1, 16)] + [place.ctx_peer(p) for p in range(1, 8)]
    greet(partners)
    for load in r.stage_loads + r.loads:
        load.start()
    forward_phase(place, r, partners)
    backward_phase(place, r)
    for copy in out_copies:
        copy.wait()
    for goal, hbm, sems in ((8, r.o_mixed, r.mixed_sems), (12, r.o_grad_states, r.states_sems)):
        for i in range(4):
            pltpu.make_async_copy(r.bgrad.at[goal + i], hbm.at[i], sems.at[i]).wait()


def layer(*arrays):
    vmem = pl.BlockSpec(memory_space=pltpu.VMEM)
    hbm = pl.BlockSpec(memory_space=pl.ANY)
    smem = pl.BlockSpec(memory_space=pltpu.SMEM)
    return pl.pallas_call(
        layer_kernel,
        out_shape=[jax.ShapeDtypeStruct(*spec) for spec in OUTPUTS.values()],
        in_specs=[vmem] * 3 + [smem] + [hbm] * 6,
        out_specs=[hbm] * 6 + [vmem],
        scratch_shapes=list(scratch_table().values()),
        compiler_params=pltpu.CompilerParams(
            collective_id=0, has_side_effects=True, vmem_limit_bytes=VMEM_LIMIT
        ),
        name="layer",
    )(*arrays)


VMEM_LIMIT = 63 << 20


def hand_out_kernel(*refs):
    srcs, small, dsts, gain, router = refs[:6], refs[6], refs[7:13], refs[13], refs[14]
    held, come, go = refs[15:21], refs[21], refs[22]
    loads = [pltpu.make_async_copy(s, h, come.at[i]) for i, (s, h) in enumerate(zip(srcs, held))]
    stores = [pltpu.make_async_copy(h, d, go.at[i]) for i, (h, d) in enumerate(zip(held, dsts))]
    for load in loads:
        load.start()
    gain[...] = small[0:1]
    router[...] = small[1:2]
    for load, store in zip(loads, stores):
        load.wait()
        store.start()
    for store in stores:
        store.wait()


def hand_out(*arrays):
    hbm = pl.BlockSpec(memory_space=pltpu.HBM)
    vmem = pl.BlockSpec(memory_space=pltpu.VMEM)
    line = jax.ShapeDtypeStruct((1, 256), F32)
    return pl.pallas_call(
        hand_out_kernel,
        out_shape=[jax.ShapeDtypeStruct(a.shape, a.dtype) for a in arrays[:6]] + [line, line],
        in_specs=[hbm] * 6 + [vmem],
        out_specs=[hbm] * 6 + [vmem] * 2,
        scratch_shapes=[vm(a.shape, a.dtype) for a in arrays[:6]] + [DMA((6,)), DMA((6,))],
        compiler_params=pltpu.CompilerParams(vmem_limit_bytes=60 << 20),
        name="hand_out",
    )(*arrays)


def body(
    states, picked, counts, norm_gain, router_weight, w_query, w_key, w_value, w_out, upstream
):
    mixed, grad_states, grad_q, grad_k, grad_v, grad_out, small = layer(
        picked,
        norm_gain,
        router_weight,
        counts,
        states.reshape(4, 2, 256, 256),
        upstream.reshape(4, 2, 256, 256),
        w_query.reshape(16, 256, 256),
        w_key.reshape(16, 256, 256),
        w_value.reshape(16, 256, 256),
        w_out,
    )
    *outs, grad_gain, grad_router = hand_out(
        mixed.reshape(states.shape),
        grad_states.reshape(states.shape),
        grad_q,
        grad_k,
        grad_v,
        grad_out,
        small,
    )
    return (*outs, grad_gain.reshape(256), grad_router.reshape(256))


def solution(mesh):
    placed = (
        P("ctx", "tp"),
        P("ctx"),
        P("ctx"),
        P("tp"),
        P("tp"),
        P(None, "tp"),
        P(None, "tp"),
        P(None, "tp"),
        P("tp", None),
        P("ctx", "tp"),
    )
    return jax.shard_map(
        body,
        mesh=mesh,
        in_specs=placed,
        out_specs=(
            P("ctx", "tp"),
            P("ctx", "tp"),
            P("ctx", "tp"),
            P("ctx", "tp"),
            P("ctx", "tp"),
            P(("tp", "ctx"), None),
            P("tp"),
            P("tp"),
        ),
        check_vma=False,
    )
```
